32 devices in a mesh: slab: 1, il: 32 (over z, y, x, core).
Axes of the slice: x: 2, y: 2, z: 4, core: 2. Of those that a mesh axis runs over, the one named last changes fastest.
Arguments:
- data: float32 [512, 128, 256], P(('slab', 'il')), may hold values from -100 to 100
- model: float32 [512, 128, 256], P(('slab', 'il')), may hold values from -6 to 6
- dip: int32 [512, 128, 256], P(('slab', 'il')), may hold values from 0 to 32
Outputs:
- new_model: float32 [512, 128, 256], P(('slab', 'il'))
- new_residual: float32 [512, 128, 256], P(('slab', 'il'))
The draws below stay inside these ranges and needn't reach their ends.
All inputs are finite; a program needn't handle non-finite values.
Results may differ from the reference program's by a relative error of at most 0.000062.
Values sent between devices are 32-bit elements; how exact they have to be, the bound alone decides.
A program may use at most 128 MiB of HBM per device.

```python
import math
import jax
import jax.numpy as jnp
from jax import lax

XL = 128
TS = 256
RAD = 64
NBINS = 33
IL = 512


def draw_data(key, part):
    key = jax.random.fold_in(key, 7)
    first = jax.random.fold_in(key, 0)
    ramp = jnp.arange(IL, dtype=jnp.float32) / (IL - 1)
    base = jax.random.truncated_normal(first, -6.0, 6.0, (IL, XL, TS), jnp.float32)
    return (base * jnp.exp(math.log(3.0) * ramp)[:, None, None]).astype(jnp.float32)


def touch_ends(drawn, own_key, low, largest):
    index_at = [jax.random.randint(jax.random.fold_in(own_key, axis), (), 0, length) for axis, length in enumerate(drawn.shape)]
    longest = drawn.shape.index(max(drawn.shape))
    next_to = index_at[:longest] + [(index_at[longest] + 1) % drawn.shape[longest]] + index_at[longest + 1:]
    return drawn.at[tuple(index_at)].set(low).at[tuple(next_to)].set(largest)


def steps_of(key, extent, pieces, smallest, high):
    level, own = 1.0, jax.random.fold_in(key, 6)
    for dim, shards_of in pieces:
        steps = jnp.exp(jax.random.uniform(jax.random.fold_in(own, dim), (shards_of,), jnp.float32, smallest / len(pieces), high / len(pieces)))
        level = level * jnp.repeat(steps, extent[dim] // shards_of).reshape([-1 if axis == dim else 1 for axis in range(len(extent))])
    return level


def centred(own_key, shape, scale, reach, cuts=(), kind=jnp.bfloat16):
    array = scale * jax.random.normal(own_key, shape, jnp.float32)
    if cuts:
        array = array * steps_of(own_key, shape, cuts, -0.22, 0.18)
    return jnp.clip(array, -reach, reach).astype(kind)


def setup_inputs(seed: int = 0, part: int = 0) -> dict:
    key_of = jax.random.split(jax.random.key(seed), 4)
    part_splits = jax.random.split(jax.random.fold_in(key_of[3], part), 4)
    return {
        "data": draw_data(jax.random.fold_in(jax.random.fold_in(key_of[3], part), 71), part),
        "model": centred(part_splits[1], (IL, XL, TS), 1.0, 6.0, ((0, 32),), jnp.float32),
        "dip": touch_ends(jax.random.randint(part_splits[2], (IL, XL, TS), 0, NBINS), jax.random.fold_in(part_splits[2], 1), 0, NBINS - 1).astype(jnp.int32),
    }


block_rows = 128

def tent(offset):
    gap = jnp.abs(offset).astype(jnp.float32)
    return jnp.where(gap < RAD, (RAD - gap) / (RAD * RAD), 0.0).astype(jnp.float32)

def smooth_rows(volume):
    count = volume.shape[0]
    blocks = volume.reshape(count // block_rows, block_rows, -1)
    padded = jnp.pad(blocks, ((1, 1), (0, 0), (0, 0)))
    windows = jnp.concatenate([padded[:-2], padded[1:-1], padded[2:]], axis=1)
    out_rows = jnp.arange(block_rows)[:, None]
    in_rows = jnp.arange(3 * block_rows)[None, :]
    weights = tent(out_rows + block_rows - in_rows)
    smooth = jnp.einsum('rc,bcx->brx', weights, windows, precision=lax.Precision.HIGHEST)
    return smooth.reshape(volume.shape)

def smooth_columns(volume):
    places = jnp.arange(volume.shape[1])
    weights = tent(places[:, None] - places[None, :])
    return jnp.einsum('xy,iyt->ixt', weights, volume, precision=lax.Precision.HIGHEST)

def coefficients(slopes):
    half = (NBINS - 1) / 2.0
    slope = (slopes.astype(jnp.float32) - half) / half
    return (slope * (slope - 1.0) / 2.0, 1.0 - slope * slope, slope * (slope + 1.0) / 2.0)

def destruct(volume, slopes):
    weight_early, weight_now, weight_late = coefficients(slopes)
    previous = jnp.concatenate([jnp.zeros_like(volume[:1]), volume[:-1]], 0)
    earlier = jnp.pad(previous, ((0, 0), (0, 0), (1, 0)))[:, :, :-1]
    later = jnp.pad(previous, ((0, 0), (0, 0), (0, 1)))[:, :, 1:]
    return volume - (weight_early * earlier + weight_now * previous + weight_late * later)

def reference(data, model, dip):
    residual = data - destruct(model, dip)
    _, pull = jax.vjp(lambda volume: destruct(volume, dip), model)
    gradient = pull(residual)[0]
    shaped = smooth_columns(smooth_rows(gradient))
    image = destruct(shaped, dip)
    alpha = jnp.sum(gradient * shaped) / (jnp.sum(image * image) + jnp.sum(shaped * shaped))
    return (model + alpha * shaped, residual - alpha * image)
```

```python
import functools

import jax
import jax.numpy as jnp
import numpy as np
from jax import lax
from jax.experimental import pallas as pl
from jax.experimental.pallas import tpu as pltpu
from jax.sharding import PartitionSpec as P

RAD = 64
NBINS = 33
PARTS = 8


def at_lane(x, lane):
    return lax.broadcasted_iota(jnp.int32, x.shape, x.ndim - 1) == lane


def before(x):
    return jnp.where(at_lane(x, 0), 0.0, pltpu.roll(x, 1, x.ndim - 1))


def after(x):
    last = x.shape[-1] - 1
    return jnp.where(at_lane(x, last), 0.0, pltpu.roll(x, last, x.ndim - 1))


def coefficients(bins):
    half = (NBINS - 1) // 2
    slope = (bins - half).astype(jnp.float32) * (1.0 / half)
    square = slope * slope
    return 0.5 * (square - slope), 1.0 - square, 0.5 * (square + slope)


def predict(u, weights):
    early, now, late = weights
    return early * before(u) + now * u + late * after(u)


def spread(r, weights):
    early, now, late = weights
    return now * r + after(early * r) + before(late * r)


def kernel(n, data_hbm, model_hbm, dip_hbm, tents_ref, new_model, new_res,
           data, model, dip, res, grad, halo, sums_out, sums_in, split, shaped, image,
           below, above, above_dip, part, table, part_two, table_two,
           load_sem, edge_send, edge_recv, near_send, near_recv, far_send, far_recv,
           sum_send, sum_recv, one_send, one_recv, two_send, two_recv):
    count, columns, _ = data.shape
    width = columns // PARTS
    groups = n // 8
    me = lax.axis_index("il")
    pos = lax.rem(me, 8)
    group = lax.div(me, 8)
    side = lax.div(pos, 4)
    place = lax.rem(pos, 4)
    base8 = me - pos
    base4 = me - place
    toward = 1 - 2 * side
    partner = me + 4 * toward
    onward = me + 8 * toward
    origin = me - 8 * toward
    has_onward = jnp.logical_and(onward >= 0, onward < n)
    has_origin = jnp.logical_and(origin >= 0, origin < n)
    has_below = me > 0
    has_above = me < n - 1

    def remote(src, dst, send, recv, to):
        return pltpu.make_async_remote_copy(
            src_ref=src, dst_ref=dst, send_sem=send, recv_sem=recv,
            device_id={"il": to}, device_id_type=pl.DeviceIdType.MESH)

    loads = [pltpu.make_async_copy(src, dst, load_sem.at[i]) for i, (src, dst) in enumerate(
        ((data_hbm, data), (model_hbm, model), (dip_hbm, dip)))]
    for load in loads:
        load.start()

    barrier = pltpu.get_barrier_semaphore()

    def greet(other):
        pl.semaphore_signal(barrier, inc=1, device_id={"il": other},
                            device_id_type=pl.DeviceIdType.MESH)

    for o in range(1, 8):
        greet(base8 + lax.rem(pos + o, 8))
    for o in range(1, groups):
        greet(lax.rem(me + 8 * o, n))
    cross_below = jnp.logical_and(pos == 0, has_below)
    cross_above = jnp.logical_and(pos == 7, has_above)

    @pl.when(cross_below)
    def _():
        greet(me - 1)

    @pl.when(cross_above)
    def _():
        greet(me + 1)

    crossings = cross_below.astype(jnp.int32) + cross_above.astype(jnp.int32)
    pl.semaphore_wait(barrier, 7 + groups - 1 + crossings)

    def up():
        return [remote(model_hbm.at[count - 1], below, edge_send.at[0], edge_recv.at[0], me + 1)]

    def down():
        return [remote(src.at[0], dst, edge_send.at[i], edge_recv.at[i], me - 1)
                for i, src, dst in ((1, data_hbm, above.at[0]), (2, model_hbm, above.at[1]),
                                    (3, dip_hbm, above_dip))]

    @pl.when(has_above)
    def _():
        for copy in up():
            copy.start()

    @pl.when(has_below)
    def _():
        for copy in down():
            copy.start()

    for load in loads:
        load.wait()

    def strip(k):
        return pl.ds(pl.multiple_of(k * width, width), width)

    def own(k, carry):
        xs = strip(k)
        last = None
        for i in range(1, count):
            weights = coefficients(dip[i, xs])
            r = data[i, xs] - model[i, xs] + predict(model[i - 1, xs], weights)
            res[i, xs] = r
            s = spread(r, weights)
            grad[i - 1, xs] = -s if last is None else last - s
            last = r
        grad[count - 1, xs] = last
        return carry

    lax.fori_loop(0, PARTS, own, 0)

    @pl.when(has_below)
    def _():
        for copy in up():
            copy.wait_recv()

    @pl.when(jnp.logical_not(has_below))
    def _():
        below[...] = jnp.zeros_like(below)

    @pl.when(has_above)
    def _():
        for copy in down():
            copy.wait_recv()

    def edges(k, carry):
        xs = strip(k)
        r = data[0, xs] - model[0, xs] + predict(below[xs], coefficients(dip[0, xs]))
        res[0, xs] = r
        grad[0, xs] = grad[0, xs] + r

        @pl.when(has_above)
        def _():
            weights = coefficients(above_dip[xs])
            r = above[0, xs] - above[1, xs] + predict(model[count - 1, xs], weights)
            grad[count - 1, xs] = grad[count - 1, xs] - spread(r, weights)

        near(k).start()
        return carry

    def near(k):
        return remote(grad.at[:, strip(k)], halo.at[side, :, strip(k)],
                      near_send.at[k], near_recv.at[k], partner)

    def near_arrival(k):
        return remote(grad.at[:, strip(k)], halo.at[1 - side, :, strip(k)],
                      near_send.at[k], near_recv.at[k], partner)

    def far(k):
        return remote(halo.at[1 - side, :, strip(k)], halo.at[side, :, strip(k)],
                      far_send.at[k], far_recv.at[k], onward)

    def moments(o, k):
        return remote(sums_out.at[o - 1, :, strip(k)], sums_in.at[o - 1, :, strip(k)],
                      sum_send.at[o - 1, k], sum_recv.at[o - 1, k],
                      base4 + lax.rem(place + o, 4))

    lax.fori_loop(0, PARTS, edges, 0)

    @pl.when(jnp.logical_not(has_origin))
    def _():
        def clear(i, carry):
            halo[side, i] = jnp.zeros(halo.shape[2:], halo.dtype)
            return carry
        lax.fori_loop(0, count, clear, 0)

    def totals(rows):
        zero = rows[0]
        first = rows[1]
        for row in rows[2:]:
            first = first + row
        one = rows[1]
        for j in range(2, count):
            one = one + j * rows[j]
        return zero + first, one

    def send_moments(k):
        xs = strip(k)
        left0, left1 = totals([halo[0, j, xs] for j in range(count)])
        own0, own1 = totals([grad[j, xs] for j in range(count)])
        right0, right1 = totals([halo[1, j, xs] for j in range(count)])
        for o in range(1, 4):
            wrap = place + o >= 4
            a0 = jnp.where(wrap, left0, own0)
            a1 = jnp.where(wrap, left1, own1)
            b0 = jnp.where(wrap, own0, right0)
            b1 = jnp.where(wrap, own1, right1)
            sums_out[o - 1, 0, xs] = (RAD - count * o) * a0 + a1 + (count * o) * b0 - b1
            sums_out[o - 1, 1, xs] = b0 - a0
            moments(o, k).start()
        sums_out[3, 0, xs] = RAD * own0 - own1 + left1
        sums_out[3, 1, xs] = own0 - left0

    def smooth(k):
        xs = strip(k)
        for o in range(1, 4):
            moments(o, k).wait_recv()
        value = sums_out[3, 0, xs]
        step = sums_out[3, 1, xs]
        for o in range(3):
            value = value + sums_in[o, 0, xs]
            step = step + sums_in[o, 1, xs]
        low = pl.ds(pl.multiple_of(columns + k * width, width), width)

        def put(i, v):
            high = v.astype(jnp.bfloat16)
            split[i, xs] = high
            split[i, low] = (v - high.astype(jnp.float32)).astype(jnp.bfloat16)

        put(0, value - step)
        for i in range(count):
            put(i + 1, value)
            if i < count - 1:
                step = step + ((halo[0, i, xs] + halo[1, i, xs]) - 2.0 * grad[i, xs])
                value = value + step

    def stage(k, carry):
        @pl.when(k < PARTS)
        def _():
            near_arrival(k).wait_recv()

            @pl.when(has_onward)
            def _():
                far(k).start()

        @pl.when(jnp.logical_and(k >= 1, k <= PARTS))
        def _():
            @pl.when(has_origin)
            def _():
                far(k - 1).wait_recv()
            send_moments(k - 1)

        @pl.when(k >= 2)
        def _():
            smooth(k - 2)
        return carry

    lax.fori_loop(0, PARTS + 2, stage, 0)

    def across(i, carry):
        out = jnp.dot(tents_ref[...], split[i], preferred_element_type=jnp.float32)
        shaped[i] = jnp.where(jnp.logical_or(i > 0, has_below), out, 0.0)
        return carry

    lax.fori_loop(0, count + 1, across, 0)

    def fold(x):
        return jnp.sum(x.reshape(x.shape[0] // 8, 8, x.shape[1]), 0)

    def images(k, carry):
        xs = strip(k)
        along, energy, length = carry
        last = shaped[0, xs]
        for i in range(count):
            now = shaped[i + 1, xs]
            im = now - predict(last, coefficients(dip[i, xs]))
            image[i, xs] = im
            along = along + fold(grad[i, xs] * now)
            energy = energy + fold(im * im)
            length = length + fold(now * now)
            last = now
        return along, energy, length

    none = jnp.zeros((8, data.shape[2]), jnp.float32)
    sums = lax.fori_loop(0, PARTS, images, (none, none, none))
    row = lax.broadcasted_iota(jnp.int32, (8, 128), 0)
    tile = jnp.zeros((8, 128), jnp.float32)
    for q, total in enumerate(sums):
        flat = jnp.sum(total, 0, keepdims=True)
        flat = sum(flat[:, c:c + 128] for c in range(0, flat.shape[1], 128))
        tile = jnp.where(row == q, flat, tile)
    part[...] = tile
    table[pos] = tile

    def one(o):
        return remote(part, table.at[pos], one_send.at[o - 1], one_recv.at[o - 1],
                      base8 + lax.rem(pos + o, 8))

    def one_arrival(o):
        return remote(part, table.at[lax.rem(pos + 8 - o, 8)], one_send.at[o - 1],
                      one_recv.at[o - 1], base8 + lax.rem(pos + o, 8))

    def two(o):
        return remote(part_two, table_two.at[group], two_send.at[o - 1], two_recv.at[o - 1],
                      lax.rem(me + 8 * o, n))

    def two_arrival(o):
        return remote(part_two, table_two.at[lax.rem(group + groups - o, groups)],
                      two_send.at[o - 1], two_recv.at[o - 1], lax.rem(me + 8 * o, n))

    for o in range(1, 8):
        one(o).start()
    for o in range(1, 8):
        one_arrival(o).wait_recv()
    tile = table[0]
    for o in range(1, 8):
        tile = tile + table[o]
    part_two[...] = tile
    table_two[group] = tile
    for o in range(1, groups):
        two(o).start()
    for o in range(1, groups):
        two_arrival(o).wait_recv()
    tile = table_two[0]
    for o in range(1, groups):
        tile = tile + table_two[o]
    along, energy, length = (jnp.sum(tile[q:q + 1], 1, keepdims=True) for q in range(3))
    alpha = along / (energy + length)

    def update(i, carry):
        new_model[i] = model[i] + alpha * shaped[i + 1]
        new_res[i] = res[i] - alpha * image[i]
        return carry

    lax.fori_loop(0, count, update, 0)

    @pl.when(has_above)
    def _():
        for copy in up():
            copy.wait_send()

    @pl.when(has_below)
    def _():
        for copy in down():
            copy.wait_send()

    def finish(k, carry):
        near(k).wait_send()

        @pl.when(has_onward)
        def _():
            far(k).wait_send()
        for o in range(1, 4):
            moments(o, k).wait_send()
        return carry

    lax.fori_loop(0, PARTS, finish, 0)
    for o in range(1, 8):
        one(o).wait_send()
    for o in range(1, groups):
        two(o).wait_send()


def local(n, data, model, dip):
    count, columns, times = data.shape
    assert count * 4 == RAD and n % 8 == 0
    groups = n // 8
    gap = np.abs(np.arange(columns)[:, None] - np.arange(columns)[None, :])
    tent = np.maximum(RAD - gap, 0) / float(RAD) ** 4
    tents = jnp.asarray(np.concatenate([tent, tent], 1), jnp.bfloat16)
    block = (count, columns, times)
    f32 = jnp.float32
    dma = pltpu.SemaphoreType.DMA
    return pl.pallas_call(
        functools.partial(kernel, n),
        out_shape=[jax.ShapeDtypeStruct(block, f32)] * 2,
        in_specs=[pl.BlockSpec(memory_space=pl.ANY)] * 3
        + [pl.BlockSpec(memory_space=pltpu.VMEM)],
        out_specs=[pl.BlockSpec(memory_space=pltpu.VMEM)] * 2,
        scratch_shapes=[
            pltpu.VMEM(block, f32),
            pltpu.VMEM(block, f32),
            pltpu.VMEM(block, jnp.int32),
            pltpu.VMEM(block, f32),
            pltpu.VMEM(block, f32),
            pltpu.VMEM((2,) + block, f32),
            pltpu.VMEM((4, 2, columns, times), f32),
            pltpu.VMEM((3, 2, columns, times), f32),
            pltpu.VMEM((count + 1, 2 * columns, times), jnp.bfloat16),
            pltpu.VMEM((count + 1, columns, times), f32),
            pltpu.VMEM(block, f32),
            pltpu.VMEM((columns, times), f32),
            pltpu.VMEM((2, columns, times), f32),
            pltpu.VMEM((columns, times), jnp.int32),
            pltpu.VMEM((8, 128), f32),
            pltpu.VMEM((8, 8, 128), f32),
            pltpu.VMEM((8, 128), f32),
            pltpu.VMEM((groups, 8, 128), f32),
            dma((3,)),
            dma((4,)), dma((4,)),
            dma((PARTS,)), dma((PARTS,)),
            dma((PARTS,)), dma((PARTS,)),
            dma((3, PARTS)), dma((3, PARTS)),
            dma((7,)), dma((7,)),
            dma((max(groups - 1, 1),)), dma((max(groups - 1, 1),)),
        ],
        compiler_params=pltpu.CompilerParams(
            collective_id=0, has_side_effects=True, vmem_limit_bytes=48 * 2**20),
    )(data, model, dip, tents)


def solution(mesh):
    placed = P(("slab", "il"), None, None)
    return jax.shard_map(
        functools.partial(local, mesh.shape["il"]),
        mesh=mesh,
        in_specs=(placed, placed, placed),
        out_specs=(placed, placed),
        check_vma=False,
    )
```

```python
import functools

import jax
import jax.numpy as jnp
from jax import lax
from jax.experimental import pallas as pl
from jax.experimental.pallas import tpu as pltpu
from jax.sharding import PartitionSpec as P

RAD = 64
NBINS = 33
PARTS = 8
GROUP = 8
EARLY = 1
PIECES = 4


def pieces(count):
    third = (count - 2 + 2) // 3
    return ((2, third), (2 + third, third), (2 + 2 * third, count - 2 - 2 * third), (0, 2))


def at_lane(x, lane):
    return lax.broadcasted_iota(jnp.int32, x.shape, x.ndim - 1) == lane


def before(x):
    return jnp.where(at_lane(x, 0), 0.0, pltpu.roll(x, 1, x.ndim - 1))


def after(x):
    last = x.shape[-1] - 1
    return jnp.where(at_lane(x, last), 0.0, pltpu.roll(x, last, x.ndim - 1))


def coefficients(bins):
    half = (NBINS - 1) // 2
    slope = (bins - half).astype(jnp.float32) * (1.0 / half)
    square = slope * slope
    return 0.5 * (square - slope), 1.0 - square, 0.5 * (square + slope)


def predict(u, weights):
    early, now, late = weights
    return early * before(u) + now * u + late * after(u)


def spread(r, weights):
    early, now, late = weights
    return now * r + after(early * r) + before(late * r)


def kernel(n, data_hbm, model_hbm, dip_hbm, new_model, new_res,
           data, model, dip, res, grad, halo, sums_out, sums_in, split, tents, tents_last, shaped, image,
           below, above, above_dip, part, table, part_two, table_two,
           load_sem, edge_send, edge_recv, near_send, near_recv, far_send, far_recv,
           sum_send, sum_recv, one_send, one_recv, two_send, two_recv):
    count, columns, _ = data.shape
    cuts = pieces(count)

    def slot(i):
        return (i + 1) % count

    width = columns // PARTS
    size = min(GROUP, n)
    groups = n // size
    me = lax.axis_index("il")
    pos = lax.rem(me, size)
    group = lax.div(me, size)
    side = lax.rem(lax.div(me, 4), 2)
    place = lax.rem(me, 4)
    base = me - pos
    base4 = me - place
    toward = 1 - 2 * side
    partner = me + 4 * toward
    onward = me + 8 * toward
    origin = me - 8 * toward
    has_onward = jnp.logical_and(onward >= 0, onward < n)
    has_origin = jnp.logical_and(origin >= 0, origin < n)
    has_below = me > 0
    has_above = me < n - 1

    def remote(src, dst, send, recv, to):
        return pltpu.make_async_remote_copy(
            src_ref=src, dst_ref=dst, send_sem=send, recv_sem=recv,
            device_id={"il": to}, device_id_type=pl.DeviceIdType.MESH)

    loads = [pltpu.make_async_copy(src, dst, load_sem.at[i]) for i, (src, dst) in enumerate(
        ((data_hbm, data), (model_hbm, model), (dip_hbm, dip)))]
    for load in loads:
        load.start()

    barrier = pltpu.get_barrier_semaphore()

    def greet(other):
        pl.semaphore_signal(barrier, inc=1, device_id={"il": other},
                            device_id_type=pl.DeviceIdType.MESH)

    for o in range(1, size):
        greet(base + lax.rem(pos + o, size))
    for o in range(1, groups):
        greet(lax.rem(me + size * o, n))
    cross_below = jnp.logical_and(pos == 0, has_below)
    cross_above = jnp.logical_and(pos == size - 1, has_above)

    @pl.when(cross_below)
    def _():
        greet(me - 1)

    @pl.when(cross_above)
    def _():
        greet(me + 1)

    crossings = cross_below.astype(jnp.int32) + cross_above.astype(jnp.int32)
    pl.semaphore_wait(barrier, size - 1 + groups - 1 + crossings)

    def up():
        return [remote(model_hbm.at[count - 1], below, edge_send.at[0], edge_recv.at[0], me + 1)]

    def down():
        return [remote(src.at[0], dst, edge_send.at[i], edge_recv.at[i], me - 1)
                for i, src, dst in ((1, data_hbm, above.at[0]), (2, model_hbm, above.at[1]),
                                    (3, dip_hbm, above_dip))]

    @pl.when(has_above)
    def _():
        for copy in up():
            copy.start()

    @pl.when(has_below)
    def _():
        for copy in down():
            copy.start()

    def tent_weights(first, shape):
        row = lax.broadcasted_iota(jnp.int32, shape, 0)
        lane = lax.broadcasted_iota(jnp.int32, shape, 1) + first
        column = (lane // (2 * width)) * width + lane % width
        weight = jnp.maximum(RAD - jnp.abs(row - column), 0).astype(jnp.float32)
        return (weight * (1.0 / float(RAD) ** 4)).astype(jnp.bfloat16)

    last_strip = 2 * (columns - width)
    tents[...] = tent_weights(0, tents.shape)
    tents_last[...] = tent_weights(last_strip, tents_last.shape)
    for i in range(count + 1):
        split[i, pl.ds(last_strip, 2 * width)] = jnp.zeros((2 * width, split.shape[2]), split.dtype)

    for load in loads:
        load.wait()

    def strip(k):
        return pl.ds(pl.multiple_of(k * width, width), width)

    def rows(h):
        return pl.ds(*cuts[h])

    def near(k, h):
        return remote(grad.at[rows(h), strip(k)], halo.at[side, rows(h), strip(k)],
                      near_send.at[k, h], near_recv.at[k, h], partner)

    def near_arrival(k, h):
        return remote(grad.at[rows(h), strip(k)], halo.at[1 - side, rows(h), strip(k)],
                      near_send.at[k, h], near_recv.at[k, h], partner)

    def far(k, h):
        return remote(halo.at[1 - side, rows(h), strip(k)], halo.at[side, rows(h), strip(k)],
                      far_send.at[k, h], far_recv.at[k, h], onward)

    def moments(o, k):
        return remote(sums_out.at[o - 1, :, strip(k)], sums_in.at[o - 1, :, strip(k)],
                      sum_send.at[o - 1, k], sum_recv.at[o - 1, k],
                      base4 + lax.rem(place + o, 4))

    def own(k, carry):
        xs = strip(k)
        last = None
        for i in range(1, count):
            weights = coefficients(dip[i, xs])
            r = data[i, xs] - model[i, xs] + predict(model[i - 1, xs], weights)
            res[i, xs] = r
            s = spread(r, weights)
            grad[slot(i - 1), xs] = -s if last is None else last - s
            last = r
        grad[slot(count - 1), xs] = last

        @pl.when(k < EARLY)
        def _():
            for h in range(PIECES - 1):
                near(k, h).start()
        return carry

    lax.fori_loop(0, PARTS, own, 0)

    @pl.when(has_below)
    def _():
        for copy in up():
            copy.wait_recv()

    @pl.when(jnp.logical_not(has_below))
    def _():
        below[...] = jnp.zeros_like(below)

    @pl.when(has_above)
    def _():
        for copy in down():
            copy.wait_recv()

    def edges(k, carry):
        xs = strip(k)
        r = data[0, xs] - model[0, xs] + predict(below[xs], coefficients(dip[0, xs]))
        res[0, xs] = r
        grad[slot(0), xs] = grad[slot(0), xs] + r

        @pl.when(has_above)
        def _():
            weights = coefficients(above_dip[xs])
            r = above[0, xs] - above[1, xs] + predict(model[count - 1, xs], weights)
            grad[slot(count - 1), xs] = grad[slot(count - 1), xs] - spread(r, weights)

        near(k, PIECES - 1).start()

        @pl.when(k >= EARLY)
        def _():
            for h in range(PIECES - 1):
                near(k, h).start()
        return carry

    lax.fori_loop(0, PARTS, edges, 0)

    @pl.when(jnp.logical_not(has_origin))
    def _():
        def clear(i, carry):
            halo[side, i] = jnp.zeros(halo.shape[2:], halo.dtype)
            return carry
        lax.fori_loop(0, count, clear, 0)

    def totals(rows):
        zero = rows[0]
        first = rows[1]
        for row in rows[2:]:
            first = first + row
        one = rows[1]
        for j in range(2, count):
            one = one + j * rows[j]
        return zero + first, one

    def send_moments(k):
        xs = strip(k)
        left0, left1 = totals([halo[0, slot(j), xs] for j in range(count)])
        own0, own1 = totals([grad[slot(j), xs] for j in range(count)])
        right0, right1 = totals([halo[1, slot(j), xs] for j in range(count)])
        for o in range(1, 4):
            wrap = place + o >= 4
            a0 = jnp.where(wrap, left0, own0)
            a1 = jnp.where(wrap, left1, own1)
            b0 = jnp.where(wrap, own0, right0)
            b1 = jnp.where(wrap, own1, right1)
            sums_out[o - 1, 0, xs] = (RAD - count * o) * a0 + a1 + (count * o) * b0 - b1
            sums_out[o - 1, 1, xs] = b0 - a0
            moments(o, k).start()
        sums_out[3, 0, xs] = RAD * own0 - own1 + left1
        sums_out[3, 1, xs] = own0 - left0

    def smooth(k):
        xs = strip(k)
        for o in range(1, 4):
            moments(o, k).wait_recv()
        value = sums_out[3, 0, xs]
        step = sums_out[3, 1, xs]
        for o in range(3):
            value = value + sums_in[o, 0, xs]
            step = step + sums_in[o, 1, xs]
        top = pl.ds(pl.multiple_of(2 * k * width, width), width)
        low = pl.ds(pl.multiple_of((2 * k + 1) * width, width), width)

        def put(i, v):
            high = v.astype(jnp.bfloat16)
            split[i, top] = high
            split[i, low] = (v - high.astype(jnp.float32)).astype(jnp.bfloat16)

        put(0, value - step)
        for i in range(count):
            put(i + 1, value)
            if i < count - 1:
                step = step + ((halo[0, slot(i), xs] + halo[1, slot(i), xs]) - 2.0 * grad[slot(i), xs])
                value = value + step

    def stage(k, carry):
        @pl.when(k < PARTS)
        def _():
            for h in range(PIECES):
                near_arrival(k, h).wait_recv()

                @pl.when(has_onward)
                def _():
                    far(k, h).start()

        @pl.when(jnp.logical_and(k >= 1, k <= PARTS))
        def _():
            @pl.when(has_origin)
            def _():
                for h in range(PIECES):
                    far(k - 1, h).wait_recv()
            send_moments(k - 1)

        @pl.when(k >= 2)
        def _():
            smooth(k - 2)
        return carry

    lax.fori_loop(0, PARTS + 1, stage, 0)

    def across(i, carry):
        shaped[i] = jnp.dot(tents[...], split[i], preferred_element_type=jnp.float32)
        return carry

    lax.fori_loop(0, count + 1, across, 0, unroll=True)
    smooth(PARTS - 1)

    def across_last(i, carry):
        more = jnp.dot(tents_last[...], split[i, pl.ds(last_strip, 2 * width)],
                       preferred_element_type=jnp.float32)
        out = shaped[i] + more
        shaped[i] = jnp.where(jnp.logical_or(i > 0, has_below), out, 0.0)
        return carry

    lax.fori_loop(0, count + 1, across_last, 0, unroll=True)

    def fold(x):
        return jnp.sum(x.reshape(x.shape[0] // 8, 8, x.shape[1]), 0)

    def images(k, carry):
        xs = strip(k)
        along, energy, length = carry
        last = shaped[0, xs]
        for i in range(count):
            now = shaped[i + 1, xs]
            im = now - predict(last, coefficients(dip[i, xs]))
            image[i, xs] = im
            along = along + fold(grad[slot(i), xs] * now)
            energy = energy + fold(im * im)
            length = length + fold(now * now)
            last = now
        return along, energy, length

    none = jnp.zeros((8, data.shape[2]), jnp.float32)
    sums = lax.fori_loop(0, PARTS, images, (none, none, none))
    row = lax.broadcasted_iota(jnp.int32, (8, 128), 0)
    tile = jnp.zeros((8, 128), jnp.float32)
    for q, total in enumerate(sums):
        flat = jnp.sum(total, 0, keepdims=True)
        flat = sum(flat[:, c:c + 128] for c in range(0, flat.shape[1], 128))
        tile = jnp.where(row == q, flat, tile)
    part[...] = tile
    table[pos] = tile

    def one(o):
        return remote(part, table.at[pos], one_send.at[o - 1], one_recv.at[o - 1],
                      base + lax.rem(pos + o, size))

    def one_arrival(o):
        return remote(part, table.at[lax.rem(pos + size - o, size)], one_send.at[o - 1],
                      one_recv.at[o - 1], base + lax.rem(pos + o, size))

    def two(o):
        return remote(part_two, table_two.at[group], two_send.at[o - 1], two_recv.at[o - 1],
                      lax.rem(me + size * o, n))

    def two_arrival(o):
        return remote(part_two, table_two.at[lax.rem(group + groups - o, groups)],
                      two_send.at[o - 1], two_recv.at[o - 1], lax.rem(me + size * o, n))

    for o in range(1, size):
        one(o).start()
    for o in range(1, size):
        one_arrival(o).wait_recv()
    tile = table[0]
    for o in range(1, size):
        tile = tile + table[o]
    part_two[...] = tile
    table_two[group] = tile
    for o in range(1, groups):
        two(o).start()
    for o in range(1, groups):
        two_arrival(o).wait_recv()
    tile = table_two[0]
    for o in range(1, groups):
        tile = tile + table_two[o]
    along, energy, length = (jnp.sum(tile[q:q + 1], 1, keepdims=True) for q in range(3))
    alpha = along / (energy + length)

    def update(i, carry):
        new_model[i] = model[i] + alpha * shaped[i + 1]
        new_res[i] = res[i] - alpha * image[i]
        return carry

    lax.fori_loop(0, count, update, 0)

    @pl.when(has_above)
    def _():
        for copy in up():
            copy.wait_send()

    @pl.when(has_below)
    def _():
        for copy in down():
            copy.wait_send()

    def finish(k, carry):
        for h in range(PIECES):
            near(k, h).wait_send()

        @pl.when(has_onward)
        def _():
            for h in range(PIECES):
                far(k, h).wait_send()
        for o in range(1, 4):
            moments(o, k).wait_send()
        return carry

    lax.fori_loop(0, PARTS, finish, 0)
    for o in range(1, size):
        one(o).wait_send()
    for o in range(1, groups):
        two(o).wait_send()


def local(n, data, model, dip):
    count, columns, times = data.shape
    assert count * 4 == RAD and n % 8 == 0
    size = min(GROUP, n)
    groups = n // size
    width = columns // PARTS
    block = (count, columns, times)
    f32 = jnp.float32
    dma = pltpu.SemaphoreType.DMA
    return pl.pallas_call(
        functools.partial(kernel, n),
        out_shape=[jax.ShapeDtypeStruct(block, f32)] * 2,
        in_specs=[pl.BlockSpec(memory_space=pl.ANY)] * 3,
        out_specs=[pl.BlockSpec(memory_space=pltpu.VMEM)] * 2,
        scratch_shapes=[
            pltpu.VMEM(block, f32),
            pltpu.VMEM(block, f32),
            pltpu.VMEM(block, jnp.int32),
            pltpu.VMEM(block, f32),
            pltpu.VMEM(block, f32),
            pltpu.VMEM((2,) + block, f32),
            pltpu.VMEM((4, 2, columns, times), f32),
            pltpu.VMEM((3, 2, columns, times), f32),
            pltpu.VMEM((count + 1, 2 * columns, times), jnp.bfloat16),
            pltpu.VMEM((columns, 2 * columns), jnp.bfloat16),
            pltpu.VMEM((columns, 2 * width), jnp.bfloat16),
            pltpu.VMEM((count + 1, columns, times), f32),
            pltpu.VMEM(block, f32),
            pltpu.VMEM((columns, times), f32),
            pltpu.VMEM((2, columns, times), f32),
            pltpu.VMEM((columns, times), jnp.int32),
            pltpu.VMEM((8, 128), f32),
            pltpu.VMEM((size, 8, 128), f32),
            pltpu.VMEM((8, 128), f32),
            pltpu.VMEM((groups, 8, 128), f32),
            dma((3,)),
            dma((4,)), dma((4,)),
            dma((PARTS, PIECES)), dma((PARTS, PIECES)),
            dma((PARTS, PIECES)), dma((PARTS, PIECES)),
            dma((3, PARTS)), dma((3, PARTS)),
            dma((size - 1,)), dma((size - 1,)),
            dma((max(groups - 1, 1),)), dma((max(groups - 1, 1),)),
        ],
        compiler_params=pltpu.CompilerParams(
            collective_id=0, has_side_effects=True, vmem_limit_bytes=48 * 2**20),
    )(data, model, dip)


def solution(mesh):
    placed = P(("slab", "il"), None, None)
    return jax.shard_map(
        functools.partial(local, mesh.shape["il"]),
        mesh=mesh,
        in_specs=(placed, placed, placed),
        out_specs=(placed, placed),
        check_vma=False,
    )
```

```python
import functools

import jax
import jax.numpy as jnp
from jax import lax
from jax.experimental import pallas as pl
from jax.experimental.pallas import tpu as pltpu
from jax.sharding import PartitionSpec as P

RAD = 64
NBINS = 33
PARTS = 8
GROUP = 8
EARLY = 1
PIECES = 3


def pieces(count):
    half = (count - 2) // 2
    return ((2, half), (2 + half, count - 2 - half), (0, 2))


def at_lane(x, lane):
    return lax.broadcasted_iota(jnp.int32, x.shape, x.ndim - 1) == lane


def before(x):
    return jnp.where(at_lane(x, 0), 0.0, pltpu.roll(x, 1, x.ndim - 1))


def after(x):
    last = x.shape[-1] - 1
    return jnp.where(at_lane(x, last), 0.0, pltpu.roll(x, last, x.ndim - 1))


def coefficients(bins):
    half = (NBINS - 1) // 2
    slope = (bins - half).astype(jnp.float32) * (1.0 / half)
    square = slope * slope
    return 0.5 * (square - slope), 1.0 - square, 0.5 * (square + slope)


def predict(u, weights):
    early, now, late = weights
    return early * before(u) + now * u + late * after(u)


def spread(r, weights):
    early, now, late = weights
    return now * r + after(early * r) + before(late * r)


def kernel(n, data_hbm, model_hbm, dip_hbm, new_model, new_res,
           data, model, dip, res, grad, halo, sums_out, sums_in, split, tents, tents_last, shaped, image,
           below, above, above_dip, part, table, part_two, table_two,
           load_sem, edge_send, edge_recv, near_send, near_recv, far_send, far_recv,
           sum_send, sum_recv, one_send, one_recv, two_send, two_recv):
    count, columns, _ = data.shape
    cuts = pieces(count)

    def slot(i):
        return (i + 1) % count

    width = columns // PARTS
    size = min(GROUP, n)
    groups = n // size
    me = lax.axis_index("il")
    pos = lax.rem(me, size)
    group = lax.div(me, size)
    side = lax.rem(lax.div(me, 4), 2)
    place = lax.rem(me, 4)
    base = me - pos
    base4 = me - place
    toward = 1 - 2 * side
    partner = me + 4 * toward
    onward = me + 8 * toward
    origin = me - 8 * toward
    has_onward = jnp.logical_and(onward >= 0, onward < n)
    has_origin = jnp.logical_and(origin >= 0, origin < n)
    has_below = me > 0
    has_above = me < n - 1

    def remote(src, dst, send, recv, to):
        return pltpu.make_async_remote_copy(
            src_ref=src, dst_ref=dst, send_sem=send, recv_sem=recv,
            device_id={"il": to}, device_id_type=pl.DeviceIdType.MESH)

    loads = [[pltpu.make_async_copy(src.at[:, cut], dst.at[:, cut], load_sem.at[i, j])
              for i, (src, dst) in enumerate(
                  ((data_hbm, data), (model_hbm, model), (dip_hbm, dip)))]
             for j, cut in enumerate((pl.ds(0, width), pl.ds(width, columns - width)))]
    for load in loads[0] + loads[1]:
        load.start()

    barrier = pltpu.get_barrier_semaphore()

    def greet(other):
        pl.semaphore_signal(barrier, inc=1, device_id={"il": other},
                            device_id_type=pl.DeviceIdType.MESH)

    for o in range(1, size):
        greet(base + lax.rem(pos + o, size))
    for o in range(1, groups):
        greet(lax.rem(me + size * o, n))
    cross_below = jnp.logical_and(pos == 0, has_below)
    cross_above = jnp.logical_and(pos == size - 1, has_above)

    @pl.when(cross_below)
    def _():
        greet(me - 1)

    @pl.when(cross_above)
    def _():
        greet(me + 1)

    crossings = cross_below.astype(jnp.int32) + cross_above.astype(jnp.int32)
    pl.semaphore_wait(barrier, size - 1 + groups - 1 + crossings)

    def up():
        return [remote(model_hbm.at[count - 1], below, edge_send.at[0], edge_recv.at[0], me + 1)]

    def down():
        return [remote(src.at[0], dst, edge_send.at[i], edge_recv.at[i], me - 1)
                for i, src, dst in ((1, data_hbm, above.at[0]), (2, model_hbm, above.at[1]),
                                    (3, dip_hbm, above_dip))]

    @pl.when(has_above)
    def _():
        for copy in up():
            copy.start()

    @pl.when(has_below)
    def _():
        for copy in down():
            copy.start()

    def tent_weights(first, shape):
        row = lax.broadcasted_iota(jnp.int32, shape, 0)
        lane = lax.broadcasted_iota(jnp.int32, shape, 1) + first
        column = (lane // (2 * width)) * width + lane % width
        weight = jnp.maximum(RAD - jnp.abs(row - column), 0).astype(jnp.float32)
        return (weight * (1.0 / float(RAD) ** 4)).astype(jnp.bfloat16)

    last_strip = 2 * (columns - width)
    tents[...] = tent_weights(0, tents.shape)
    tents_last[...] = tent_weights(last_strip, tents_last.shape)
    for i in range(count + 1):
        split[i, pl.ds(last_strip, 2 * width)] = jnp.zeros((2 * width, split.shape[2]), split.dtype)

    for load in loads[0]:
        load.wait()

    def strip(k):
        return pl.ds(pl.multiple_of(k * width, width), width)

    def rows(h):
        return pl.ds(*cuts[h])

    def near(k, h):
        return remote(grad.at[rows(h), strip(k)], halo.at[side, rows(h), strip(k)],
                      near_send.at[k, h], near_recv.at[k, h], partner)

    def near_arrival(k, h):
        return remote(grad.at[rows(h), strip(k)], halo.at[1 - side, rows(h), strip(k)],
                      near_send.at[k, h], near_recv.at[k, h], partner)

    def far(k, h):
        return remote(halo.at[1 - side, rows(h), strip(k)], halo.at[side, rows(h), strip(k)],
                      far_send.at[k, h], far_recv.at[k, h], onward)

    def moments(o, k):
        return remote(sums_out.at[o - 1, :, strip(k)], sums_in.at[o - 1, :, strip(k)],
                      sum_send.at[o - 1, k], sum_recv.at[o - 1, k],
                      base4 + lax.rem(place + o, 4))

    def own(k, carry):
        xs = strip(k)
        last = None
        for i in range(1, count):
            weights = coefficients(dip[i, xs])
            r = data[i, xs] - model[i, xs] + predict(model[i - 1, xs], weights)
            res[i, xs] = r
            s = spread(r, weights)
            grad[slot(i - 1), xs] = -s if last is None else last - s
            last = r
        grad[slot(count - 1), xs] = last

        @pl.when(jnp.int32(k) < EARLY)
        def _():
            for h in range(PIECES - 1):
                near(k, h).start()
        return carry

    own(0, 0)
    for load in loads[1]:
        load.wait()
    lax.fori_loop(1, PARTS, own, 0)

    @pl.when(has_below)
    def _():
        for copy in up():
            copy.wait_recv()

    @pl.when(jnp.logical_not(has_below))
    def _():
        below[...] = jnp.zeros_like(below)

    @pl.when(has_above)
    def _():
        for copy in down():
            copy.wait_recv()

    def edges(k, carry):
        xs = strip(k)
        r = data[0, xs] - model[0, xs] + predict(below[xs], coefficients(dip[0, xs]))
        res[0, xs] = r
        grad[slot(0), xs] = grad[slot(0), xs] + r

        @pl.when(has_above)
        def _():
            weights = coefficients(above_dip[xs])
            r = above[0, xs] - above[1, xs] + predict(model[count - 1, xs], weights)
            grad[slot(count - 1), xs] = grad[slot(count - 1), xs] - spread(r, weights)

        near(k, PIECES - 1).start()

        @pl.when(k >= EARLY)
        def _():
            for h in range(PIECES - 1):
                near(k, h).start()
        return carry

    lax.fori_loop(0, PARTS, edges, 0)

    @pl.when(jnp.logical_not(has_origin))
    def _():
        def clear(i, carry):
            halo[side, i] = jnp.zeros(halo.shape[2:], halo.dtype)
            return carry
        lax.fori_loop(0, count, clear, 0)

    def totals(rows):
        zero = rows[0]
        first = rows[1]
        for row in rows[2:]:
            first = first + row
        one = rows[1]
        for j in range(2, count):
            one = one + j * rows[j]
        return zero + first, one

    def send_moments(k):
        xs = strip(k)
        left0, left1 = totals([halo[0, slot(j), xs] for j in range(count)])
        own0, own1 = totals([grad[slot(j), xs] for j in range(count)])
        right0, right1 = totals([halo[1, slot(j), xs] for j in range(count)])
        for o in range(1, 4):
            wrap = place + o >= 4
            a0 = jnp.where(wrap, left0, own0)
            a1 = jnp.where(wrap, left1, own1)
            b0 = jnp.where(wrap, own0, right0)
            b1 = jnp.where(wrap, own1, right1)
            sums_out[o - 1, 0, xs] = (RAD - count * o) * a0 + a1 + (count * o) * b0 - b1
            sums_out[o - 1, 1, xs] = b0 - a0
            moments(o, k).start()
        sums_out[3, 0, xs] = RAD * own0 - own1 + left1
        sums_out[3, 1, xs] = own0 - left0

    def smooth(k):
        xs = strip(k)
        for o in range(1, 4):
            moments(o, k).wait_recv()
        value = sums_out[3, 0, xs]
        step = sums_out[3, 1, xs]
        for o in range(3):
            value = value + sums_in[o, 0, xs]
            step = step + sums_in[o, 1, xs]
        top = pl.ds(pl.multiple_of(2 * k * width, width), width)
        low = pl.ds(pl.multiple_of((2 * k + 1) * width, width), width)

        def put(i, v):
            high = v.astype(jnp.bfloat16)
            split[i, top] = high
            split[i, low] = (v - high.astype(jnp.float32)).astype(jnp.bfloat16)

        put(0, value - step)
        for i in range(count):
            put(i + 1, value)
            if i < count - 1:
                step = step + ((halo[0, slot(i), xs] + halo[1, slot(i), xs]) - 2.0 * grad[slot(i), xs])
                value = value + step

    def stage(k, carry):
        @pl.when(k < PARTS)
        def _():
            for h in range(PIECES):
                near_arrival(k, h).wait_recv()

                @pl.when(has_onward)
                def _():
                    far(k, h).start()

        @pl.when(jnp.logical_and(k >= 1, k <= PARTS))
        def _():
            @pl.when(has_origin)
            def _():
                for h in range(PIECES):
                    far(k - 1, h).wait_recv()
            send_moments(k - 1)

        @pl.when(k >= 2)
        def _():
            smooth(k - 2)
        return carry

    lax.fori_loop(0, PARTS + 1, stage, 0)

    def across(i, carry):
        shaped[i] = jnp.dot(tents[...], split[i], preferred_element_type=jnp.float32)
        return carry

    lax.fori_loop(0, count + 1, across, 0, unroll=True)
    smooth(PARTS - 1)

    def across_last(i, carry):
        more = jnp.dot(tents_last[...], split[i, pl.ds(last_strip, 2 * width)],
                       preferred_element_type=jnp.float32)
        out = shaped[i] + more
        shaped[i] = jnp.where(jnp.logical_or(i > 0, has_below), out, 0.0)
        return carry

    lax.fori_loop(0, count + 1, across_last, 0, unroll=True)

    def fold(x):
        return jnp.sum(x.reshape(x.shape[0] // 8, 8, x.shape[1]), 0)

    def images(k, carry):
        xs = strip(k)
        along, energy, length = carry
        last = shaped[0, xs]
        for i in range(count):
            now = shaped[i + 1, xs]
            im = now - predict(last, coefficients(dip[i, xs]))
            image[i, xs] = im
            along = along + fold(grad[slot(i), xs] * now)
            energy = energy + fold(im * im)
            length = length + fold(now * now)
            last = now
        return along, energy, length

    none = jnp.zeros((8, data.shape[2]), jnp.float32)
    sums = lax.fori_loop(0, PARTS, images, (none, none, none), unroll=2)
    row = lax.broadcasted_iota(jnp.int32, (8, 128), 0)
    tile = jnp.zeros((8, 128), jnp.float32)
    for q, total in enumerate(sums):
        flat = jnp.sum(total, 0, keepdims=True)
        flat = sum(flat[:, c:c + 128] for c in range(0, flat.shape[1], 128))
        tile = jnp.where(row == q, flat, tile)
    part[...] = tile
    table[pos] = tile

    def one(o):
        return remote(part, table.at[pos], one_send.at[o - 1], one_recv.at[o - 1],
                      base + lax.rem(pos + o, size))

    def one_arrival(o):
        return remote(part, table.at[lax.rem(pos + size - o, size)], one_send.at[o - 1],
                      one_recv.at[o - 1], base + lax.rem(pos + o, size))

    def two(o):
        return remote(part_two, table_two.at[group], two_send.at[o - 1], two_recv.at[o - 1],
                      lax.rem(me + size * o, n))

    def two_arrival(o):
        return remote(part_two, table_two.at[lax.rem(group + groups - o, groups)],
                      two_send.at[o - 1], two_recv.at[o - 1], lax.rem(me + size * o, n))

    for o in range(1, size):
        one(o).start()
    @pl.when(has_above)
    def _():
        for copy in up():
            copy.wait_send()

    @pl.when(has_below)
    def _():
        for copy in down():
            copy.wait_send()

    def finish(k, carry):
        for h in range(PIECES):
            near(k, h).wait_send()

        @pl.when(has_onward)
        def _():
            for h in range(PIECES):
                far(k, h).wait_send()
        for o in range(1, 4):
            moments(o, k).wait_send()
        return carry

    lax.fori_loop(0, PARTS, finish, 0)
    for o in range(1, size):
        one_arrival(o).wait_recv()
    tile = table[0]
    for o in range(1, size):
        tile = tile + table[o]
    part_two[...] = tile
    table_two[group] = tile
    for o in range(1, groups):
        two(o).start()
    for o in range(1, groups):
        two_arrival(o).wait_recv()
    tile = table_two[0]
    for o in range(1, groups):
        tile = tile + table_two[o]
    along, energy, length = (jnp.sum(tile[q:q + 1], 1, keepdims=True) for q in range(3))
    alpha = along / (energy + length)

    def update(i, carry):
        new_model[i] = model[i] + alpha * shaped[i + 1]
        new_res[i] = res[i] - alpha * image[i]
        return carry

    lax.fori_loop(0, count, update, 0, unroll=4)

    for o in range(1, size):
        one(o).wait_send()
    for o in range(1, groups):
        two(o).wait_send()


def local(n, data, model, dip):
    count, columns, times = data.shape
    assert count * 4 == RAD and n % 8 == 0
    size = min(GROUP, n)
    groups = n // size
    width = columns // PARTS
    block = (count, columns, times)
    f32 = jnp.float32
    dma = pltpu.SemaphoreType.DMA
    return pl.pallas_call(
        functools.partial(kernel, n),
        out_shape=[jax.ShapeDtypeStruct(block, f32)] * 2,
        in_specs=[pl.BlockSpec(memory_space=pl.ANY)] * 3,
        out_specs=[pl.BlockSpec(memory_space=pltpu.VMEM)] * 2,
        scratch_shapes=[
            pltpu.VMEM(block, f32),
            pltpu.VMEM(block, f32),
            pltpu.VMEM(block, jnp.int32),
            pltpu.VMEM(block, f32),
            pltpu.VMEM(block, f32),
            pltpu.VMEM((2,) + block, f32),
            pltpu.VMEM((4, 2, columns, times), f32),
            pltpu.VMEM((3, 2, columns, times), f32),
            pltpu.VMEM((count + 1, 2 * columns, times), jnp.bfloat16),
            pltpu.VMEM((columns, 2 * columns), jnp.bfloat16),
            pltpu.VMEM((columns, 2 * width), jnp.bfloat16),
            pltpu.VMEM((count + 1, columns, times), f32),
            pltpu.VMEM(block, f32),
            pltpu.VMEM((columns, times), f32),
            pltpu.VMEM((2, columns, times), f32),
            pltpu.VMEM((columns, times), jnp.int32),
            pltpu.VMEM((8, 128), f32),
            pltpu.VMEM((size, 8, 128), f32),
            pltpu.VMEM((8, 128), f32),
            pltpu.VMEM((groups, 8, 128), f32),
            dma((3, 2)),
            dma((4,)), dma((4,)),
            dma((PARTS, PIECES)), dma((PARTS, PIECES)),
            dma((PARTS, PIECES)), dma((PARTS, PIECES)),
            dma((3, PARTS)), dma((3, PARTS)),
            dma((size - 1,)), dma((size - 1,)),
            dma((max(groups - 1, 1),)), dma((max(groups - 1, 1),)),
        ],
        compiler_params=pltpu.CompilerParams(
            collective_id=0, has_side_effects=True, vmem_limit_bytes=48 * 2**20),
    )(data, model, dip)


def solution(mesh):
    placed = P(("slab", "il"), None, None)
    return jax.shard_map(
        functools.partial(local, mesh.shape["il"]),
        mesh=mesh,
        in_specs=(placed, placed, placed),
        out_specs=(placed, placed),
        check_vma=False,
    )
```

```python
import functools

import jax
import jax.numpy as jnp
from jax import lax
from jax.experimental import pallas as pl
from jax.experimental.pallas import tpu as pltpu
from jax.sharding import PartitionSpec as P

RAD = 64
NBINS = 33
PARTS = 8
GROUP = 8
EARLY = 1
PIECES = 4


def pieces(count):
    third = count // 3
    return ((2, third), (2 + third, third), (2 + 2 * third, count - 2 - 2 * third), (0, 2))


def at_lane(x, lane):
    return lax.broadcasted_iota(jnp.int32, x.shape, x.ndim - 1) == lane


def before(x):
    return jnp.where(at_lane(x, 0), 0.0, pltpu.roll(x, 1, x.ndim - 1))


def after(x):
    last = x.shape[-1] - 1
    return jnp.where(at_lane(x, last), 0.0, pltpu.roll(x, last, x.ndim - 1))


def coefficients(bins):
    half = (NBINS - 1) // 2
    slope = (bins - half).astype(jnp.float32) * (1.0 / half)
    square = slope * slope
    return 0.5 * (square - slope), 1.0 - square, 0.5 * (square + slope)


def predict(u, weights):
    early, now, late = weights
    return early * before(u) + now * u + late * after(u)


def spread(r, weights):
    early, now, late = weights
    return now * r + after(early * r) + before(late * r)


def kernel(n, data_hbm, model_hbm, dip_hbm, new_model, new_res,
           data, model, dip, res, grad, halo, sums_out, sums_in, split, tents, tents_last, shaped, image,
           below, above, above_dip, part, table, part_two, table_two,
           load_sem, edge_send, edge_recv, near_send, near_recv, far_send, far_recv,
           sum_send, sum_recv, one_send, one_recv, two_send, two_recv):
    count, columns, _ = data.shape
    cuts = pieces(count)

    def slot(i):
        return (i + 1) % count

    width = columns // PARTS
    size = min(GROUP, n)
    groups = n // size
    me = lax.axis_index("il")
    pos = lax.rem(me, size)
    group = lax.div(me, size)
    side = lax.rem(lax.div(me, 4), 2)
    place = lax.rem(me, 4)
    base = me - pos
    base4 = me - place
    toward = 1 - 2 * side
    partner = me + 4 * toward
    onward = me + 8 * toward
    origin = me - 8 * toward
    has_onward = jnp.logical_and(onward >= 0, onward < n)
    has_origin = jnp.logical_and(origin >= 0, origin < n)
    has_below = me > 0
    has_above = me < n - 1

    def remote(src, dst, send, recv, to):
        return pltpu.make_async_remote_copy(
            src_ref=src, dst_ref=dst, send_sem=send, recv_sem=recv,
            device_id={"il": to}, device_id_type=pl.DeviceIdType.MESH)

    loads = [[pltpu.make_async_copy(src.at[:, cut], dst.at[:, cut], load_sem.at[i, j])
              for i, (src, dst) in enumerate(
                  ((data_hbm, data), (model_hbm, model), (dip_hbm, dip)))]
             for j, cut in enumerate((pl.ds(0, width), pl.ds(width, columns - width)))]
    for load in loads[0] + loads[1]:
        load.start()

    barrier = pltpu.get_barrier_semaphore()

    def greet(other):
        pl.semaphore_signal(barrier, inc=1, device_id={"il": other},
                            device_id_type=pl.DeviceIdType.MESH)

    for o in range(1, size):
        greet(base + lax.rem(pos + o, size))
    for o in range(1, groups):
        greet(lax.rem(me + size * o, n))
    cross_below = jnp.logical_and(pos == 0, has_below)
    cross_above = jnp.logical_and(pos == size - 1, has_above)

    @pl.when(cross_below)
    def _():
        greet(me - 1)

    @pl.when(cross_above)
    def _():
        greet(me + 1)

    crossings = cross_below.astype(jnp.int32) + cross_above.astype(jnp.int32)
    pl.semaphore_wait(barrier, size - 1 + groups - 1 + crossings)

    def up():
        return [remote(model_hbm.at[count - 1], below, edge_send.at[0], edge_recv.at[0], me + 1)]

    def down():
        return [remote(src.at[0], dst, edge_send.at[i], edge_recv.at[i], me - 1)
                for i, src, dst in ((1, data_hbm, above.at[0]), (2, model_hbm, above.at[1]),
                                    (3, dip_hbm, above_dip))]

    @pl.when(has_above)
    def _():
        for copy in up():
            copy.start()

    @pl.when(has_below)
    def _():
        for copy in down():
            copy.start()

    def tent_weights(first, shape):
        row = lax.broadcasted_iota(jnp.int32, shape, 0)
        lane = lax.broadcasted_iota(jnp.int32, shape, 1) + first
        column = (lane // (2 * width)) * width + lane % width
        weight = jnp.maximum(RAD - jnp.abs(row - column), 0).astype(jnp.float32)
        return (weight * (1.0 / float(RAD) ** 4)).astype(jnp.bfloat16)

    last_strip = 2 * (columns - width)
    tents[...] = tent_weights(0, tents.shape)
    tents_last[...] = tent_weights(last_strip, tents_last.shape)
    for i in range(count + 1):
        split[i, pl.ds(last_strip, 2 * width)] = jnp.zeros((2 * width, split.shape[2]), split.dtype)

    for load in loads[0]:
        load.wait()

    def strip(k):
        return pl.ds(pl.multiple_of(k * width, width), width)

    def rows(h):
        return pl.ds(*cuts[h])

    def near(k, h):
        return remote(grad.at[rows(h), strip(k)], halo.at[side, rows(h), strip(k)],
                      near_send.at[k, h], near_recv.at[k, h], partner)

    def near_arrival(k, h):
        return remote(grad.at[rows(h), strip(k)], halo.at[1 - side, rows(h), strip(k)],
                      near_send.at[k, h], near_recv.at[k, h], partner)

    def far(k, h):
        return remote(halo.at[1 - side, rows(h), strip(k)], halo.at[side, rows(h), strip(k)],
                      far_send.at[k, h], far_recv.at[k, h], onward)

    def moments(o, k):
        return remote(sums_out.at[o - 1, :, strip(k)], sums_in.at[o - 1, :, strip(k)],
                      sum_send.at[o - 1, k], sum_recv.at[o - 1, k],
                      base4 + lax.rem(place + o, 4))

    def own(k, carry):
        xs = strip(k)
        last = None
        for i in range(1, count):
            weights = coefficients(dip[i, xs])
            r = data[i, xs] - model[i, xs] + predict(model[i - 1, xs], weights)
            res[i, xs] = r
            s = spread(r, weights)
            grad[slot(i - 1), xs] = -s if last is None else last - s
            last = r
        grad[slot(count - 1), xs] = last

        @pl.when(jnp.int32(k) < EARLY)
        def _():
            for h in range(PIECES - 1):
                near(k, h).start()
        return carry

    own(0, 0)
    for load in loads[1]:
        load.wait()
    lax.fori_loop(1, PARTS, own, 0)

    @pl.when(has_below)
    def _():
        for copy in up():
            copy.wait_recv()

    @pl.when(jnp.logical_not(has_below))
    def _():
        below[...] = jnp.zeros_like(below)

    @pl.when(has_above)
    def _():
        for copy in down():
            copy.wait_recv()

    def edges(k, carry):
        xs = strip(k)
        r = data[0, xs] - model[0, xs] + predict(below[xs], coefficients(dip[0, xs]))
        res[0, xs] = r
        grad[slot(0), xs] = grad[slot(0), xs] + r

        @pl.when(has_above)
        def _():
            weights = coefficients(above_dip[xs])
            r = above[0, xs] - above[1, xs] + predict(model[count - 1, xs], weights)
            grad[slot(count - 1), xs] = grad[slot(count - 1), xs] - spread(r, weights)

        @pl.when(k >= EARLY)
        def _():
            for h in range(PIECES - 1):
                near(k, h).start()

        near(k, PIECES - 1).start()
        return carry

    lax.fori_loop(0, PARTS, edges, 0)

    @pl.when(jnp.logical_not(has_origin))
    def _():
        def clear(i, carry):
            halo[side, i] = jnp.zeros(halo.shape[2:], halo.dtype)
            return carry
        lax.fori_loop(0, count, clear, 0)

    def totals(rows):
        zero = rows[0]
        first = rows[1]
        for row in rows[2:]:
            first = first + row
        one = rows[1]
        for j in range(2, count):
            one = one + j * rows[j]
        return zero + first, one

    def send_moments(k):
        xs = strip(k)
        left0, left1 = totals([halo[0, slot(j), xs] for j in range(count)])
        own0, own1 = totals([grad[slot(j), xs] for j in range(count)])
        right0, right1 = totals([halo[1, slot(j), xs] for j in range(count)])
        for o in range(1, 4):
            wrap = place + o >= 4
            a0 = jnp.where(wrap, left0, own0)
            a1 = jnp.where(wrap, left1, own1)
            b0 = jnp.where(wrap, own0, right0)
            b1 = jnp.where(wrap, own1, right1)
            sums_out[o - 1, 0, xs] = (RAD - count * o) * a0 + a1 + (count * o) * b0 - b1
            sums_out[o - 1, 1, xs] = b0 - a0
            moments(o, k).start()
        sums_out[3, 0, xs] = RAD * own0 - own1 + left1
        sums_out[3, 1, xs] = own0 - left0

    def smooth(k):
        xs = strip(k)
        for o in range(1, 4):
            moments(o, k).wait_recv()
        value = sums_out[3, 0, xs]
        step = sums_out[3, 1, xs]
        for o in range(3):
            value = value + sums_in[o, 0, xs]
            step = step + sums_in[o, 1, xs]
        top = pl.ds(pl.multiple_of(2 * k * width, width), width)
        low = pl.ds(pl.multiple_of((2 * k + 1) * width, width), width)

        def put(i, v):
            high = v.astype(jnp.bfloat16)
            split[i, top] = high
            split[i, low] = (v - high.astype(jnp.float32)).astype(jnp.bfloat16)

        put(0, value - step)
        for i in range(count):
            put(i + 1, value)
            if i < count - 1:
                step = step + ((halo[0, slot(i), xs] + halo[1, slot(i), xs]) - 2.0 * grad[slot(i), xs])
                value = value + step

    def stage(k, carry):
        @pl.when(k < PARTS)
        def _():
            for h in range(PIECES):
                near_arrival(k, h).wait_recv()

                @pl.when(has_onward)
                def _():
                    far(k, h).start()

        @pl.when(jnp.logical_and(k >= 1, k <= PARTS))
        def _():
            @pl.when(has_origin)
            def _():
                for h in range(PIECES):
                    far(k - 1, h).wait_recv()
            send_moments(k - 1)

        @pl.when(k >= 2)
        def _():
            smooth(k - 2)
        return carry

    lax.fori_loop(0, PARTS + 1, stage, 0)

    def across(i, carry):
        shaped[i] = jnp.dot(tents[...], split[i], preferred_element_type=jnp.float32)
        return carry

    lax.fori_loop(0, count + 1, across, 0, unroll=True)
    smooth(PARTS - 1)

    def across_last(i, carry):
        more = jnp.dot(tents_last[...], split[i, pl.ds(last_strip, 2 * width)],
                       preferred_element_type=jnp.float32)
        out = shaped[i] + more
        shaped[i] = jnp.where(jnp.logical_or(i > 0, has_below), out, 0.0)
        return carry

    lax.fori_loop(0, count + 1, across_last, 0, unroll=True)

    def fold(x):
        return jnp.sum(x.reshape(x.shape[0] // 8, 8, x.shape[1]), 0)

    def images(k, carry):
        xs = strip(k)
        along, energy, length = carry
        last = shaped[0, xs]
        for i in range(count):
            now = shaped[i + 1, xs]
            im = now - predict(last, coefficients(dip[i, xs]))
            image[i, xs] = im
            along = along + fold(grad[slot(i), xs] * now)
            energy = energy + fold(im * im)
            length = length + fold(now * now)
            last = now
        return along, energy, length

    none = jnp.zeros((8, data.shape[2]), jnp.float32)
    sums = lax.fori_loop(0, PARTS, images, (none, none, none), unroll=2)
    row = lax.broadcasted_iota(jnp.int32, (8, 128), 0)
    tile = jnp.zeros((8, 128), jnp.float32)
    for q, total in enumerate(sums):
        flat = jnp.sum(total, 0, keepdims=True)
        flat = sum(flat[:, c:c + 128] for c in range(0, flat.shape[1], 128))
        tile = jnp.where(row == q, flat, tile)
    part[...] = tile
    table[pos] = tile

    def one(o):
        return remote(part, table.at[pos], one_send.at[o - 1], one_recv.at[o - 1],
                      base + lax.rem(pos + o, size))

    def one_arrival(o):
        return remote(part, table.at[lax.rem(pos + size - o, size)], one_send.at[o - 1],
                      one_recv.at[o - 1], base + lax.rem(pos + o, size))

    def two(o):
        return remote(part_two, table_two.at[group], two_send.at[o - 1], two_recv.at[o - 1],
                      lax.rem(me + size * o, n))

    def two_arrival(o):
        return remote(part_two, table_two.at[lax.rem(group + groups - o, groups)],
                      two_send.at[o - 1], two_recv.at[o - 1], lax.rem(me + size * o, n))

    for o in range(1, size):
        one(o).start()
    @pl.when(has_above)
    def _():
        for copy in up():
            copy.wait_send()

    @pl.when(has_below)
    def _():
        for copy in down():
            copy.wait_send()

    def finish(k, carry):
        for h in range(PIECES):
            near(k, h).wait_send()

        @pl.when(has_onward)
        def _():
            for h in range(PIECES):
                far(k, h).wait_send()
        for o in range(1, 4):
            moments(o, k).wait_send()
        return carry

    lax.fori_loop(0, PARTS, finish, 0)
    for o in range(1, size):
        one_arrival(o).wait_recv()
    tile = table[0]
    for o in range(1, size):
        tile = tile + table[o]
    part_two[...] = tile
    table_two[group] = tile
    for o in range(1, groups):
        two(o).start()
    for o in range(1, groups):
        two_arrival(o).wait_recv()
    tile = table_two[0]
    for o in range(1, groups):
        tile = tile + table_two[o]
    along, energy, length = (jnp.sum(tile[q:q + 1], 1, keepdims=True) for q in range(3))
    alpha = along / (energy + length)

    def update(i, carry):
        new_model[i] = model[i] + alpha * shaped[i + 1]
        new_res[i] = res[i] - alpha * image[i]
        return carry

    lax.fori_loop(0, count, update, 0, unroll=4)

    for o in range(1, size):
        one(o).wait_send()
    for o in range(1, groups):
        two(o).wait_send()


def local(n, data, model, dip):
    count, columns, times = data.shape
    assert count * 4 == RAD and n % 8 == 0
    size = min(GROUP, n)
    groups = n // size
    width = columns // PARTS
    block = (count, columns, times)
    f32 = jnp.float32
    dma = pltpu.SemaphoreType.DMA
    return pl.pallas_call(
        functools.partial(kernel, n),
        out_shape=[jax.ShapeDtypeStruct(block, f32)] * 2,
        in_specs=[pl.BlockSpec(memory_space=pl.ANY)] * 3,
        out_specs=[pl.BlockSpec(memory_space=pltpu.VMEM)] * 2,
        scratch_shapes=[
            pltpu.VMEM(block, f32),
            pltpu.VMEM(block, f32),
            pltpu.VMEM(block, jnp.int32),
            pltpu.VMEM(block, f32),
            pltpu.VMEM(block, f32),
            pltpu.VMEM((2,) + block, f32),
            pltpu.VMEM((4, 2, columns, times), f32),
            pltpu.VMEM((3, 2, columns, times), f32),
            pltpu.VMEM((count + 1, 2 * columns, times), jnp.bfloat16),
            pltpu.VMEM((columns, 2 * columns), jnp.bfloat16),
            pltpu.VMEM((columns, 2 * width), jnp.bfloat16),
            pltpu.VMEM((count + 1, columns, times), f32),
            pltpu.VMEM(block, f32),
            pltpu.VMEM((columns, times), f32),
            pltpu.VMEM((2, columns, times), f32),
            pltpu.VMEM((columns, times), jnp.int32),
            pltpu.VMEM((8, 128), f32),
            pltpu.VMEM((size, 8, 128), f32),
            pltpu.VMEM((8, 128), f32),
            pltpu.VMEM((groups, 8, 128), f32),
            dma((3, 2)),
            dma((4,)), dma((4,)),
            dma((PARTS, PIECES)), dma((PARTS, PIECES)),
            dma((PARTS, PIECES)), dma((PARTS, PIECES)),
            dma((3, PARTS)), dma((3, PARTS)),
            dma((size - 1,)), dma((size - 1,)),
            dma((max(groups - 1, 1),)), dma((max(groups - 1, 1),)),
        ],
        compiler_params=pltpu.CompilerParams(
            collective_id=0, has_side_effects=True, vmem_limit_bytes=48 * 2**20),
    )(data, model, dip)


def solution(mesh):
    placed = P(("slab", "il"), None, None)
    return jax.shard_map(
        functools.partial(local, mesh.shape["il"]),
        mesh=mesh,
        in_specs=(placed, placed, placed),
        out_specs=(placed, placed),
        check_vma=False,
    )
```
